32 devices in a mesh: dp: 8 (over y, x, core), seq: 4 (over z).
Axes of the slice: x: 2, y: 2, z: 4, core: 2. Of those that a mesh axis runs over, the one named last changes fastest.
Arguments:
- inputs: bfloat16 [8, 1040, 1024], P('dp', 'seq')
- cotangent: bfloat16 [8, 1040, 1024], P('dp', 'seq'), may hold values from -6 to 6
- valid_len: int32 [8], P('dp'), may hold values from 520 to 1025, as said below
- ln1_gain: bfloat16 [1024], P('dp'), may hold values from 0.099609375 to 1.8984375
- ln1_bias: bfloat16 [1024], P('dp'), may hold values from -3 to 3
- w_qkv: bfloat16 [1024, 3072], P('dp')
- b_qv: bfloat16 [2048], P('dp'), may hold values from -3 to 3
- w_out: bfloat16 [1024, 1024], P('dp'), may hold values from -2 to 2
- b_out: bfloat16 [1024], P('dp'), may hold values from -3 to 3
- ln2_gain: bfloat16 [1024], P('dp'), may hold values from 0.099609375 to 1.8984375
- ln2_bias: bfloat16 [1024], P('dp'), may hold values from -3 to 3
- w_up: bfloat16 [1024, 4096], P('dp'), may hold values from -0.1875 to 0.1875
- b_up: bfloat16 [4096], P('dp'), may hold values from -3 to 3
- w_down: bfloat16 [4096, 1024], P('dp'), may hold values from -0.09375 to 0.09375
- b_down: bfloat16 [1024], P('dp'), may hold values from -3 to 3
Outputs:
- outputs: bfloat16 [8, 1040, 1024], P('dp', 'seq')
- d_inputs: bfloat16 [8, 1040, 1024], P('dp', 'seq')
- g_ln1_gain: float32 [1024], P('dp')
- g_ln1_bias: float32 [1024], P('dp')
- g_w_qkv: float32 [1024, 3072], P('dp')
- g_b_qv: float32 [2048], P('dp')
- g_w_out: float32 [1024, 1024], P('dp')
- g_b_out: float32 [1024], P('dp')
- g_ln2_gain: float32 [1024], P('dp')
- g_ln2_bias: float32 [1024], P('dp')
- g_w_up: float32 [1024, 4096], P('dp')
- g_b_up: float32 [4096], P('dp')
- g_w_down: float32 [4096, 1024], P('dp')
- g_b_down: float32 [1024], P('dp')
The draws below stay inside these ranges and needn't reach their ends.
Inputs may be any that keep to these rules, and one draw needn't show every extreme that they name: `valid_len`: number of leading real tokens of each image; key slots at or after it are padding. Some image has exactly 1025 in every draw.
All inputs are finite; a program needn't handle non-finite values.
Results may differ from the reference program's by a relative error of at most 0.012.
The reference program's roundings to bfloat16 on the way count: a program that leaves them out, or rounds other values in their place, can miss the bound.
Values may be sent and summed in bfloat16 or wider, within the bound.
A program may use at most 192 MiB of HBM per device.

```python
import math
import jax
import jax.numpy as jnp
from jax import lax

D = 1024
H = 16
HD = 64
FF = 4096
LEN = 1040
VALID = 1025
IMAGES = 8


def draw_inputs(key, part):
    first_key = jax.random.fold_in(key, 0)
    return jax.random.normal(first_key, (IMAGES, LEN, D), jnp.float32).astype(jnp.bfloat16)


def draw_w_qkv(key, part):
    base = jax.random.normal(key, (D, 3 * D), jnp.float32) * (1.0 / D ** 0.5)
    return base.astype(jnp.bfloat16)


def draw_valid_len(key, part):
    drawn = jax.random.randint(key, (IMAGES,), LEN // 2, VALID + 1, dtype=jnp.int32)
    return drawn.at[0].set(VALID)


def shard_levels(key, shape, pieces, least, high):
    def one(position, parts):
        draws = jax.random.uniform(jax.random.fold_in(jax.random.fold_in(key, 6), position), (parts,), jnp.float32, least / len(pieces), high / len(pieces))
        return jnp.repeat(jnp.exp(draws), shape[position] // parts).reshape((-1,) + (1,) * (len(shape) - position - 1))

    gain = one(*pieces[0])
    for cut in pieces[1:]:
        gain = gain * one(*cut)
    return gain


def gaussian(key, shape, width, bound, cuts=(), kind=jnp.bfloat16):
    entries = jax.random.normal(key, shape, jnp.float32) * width
    if len(cuts) > 0:
        entries = shard_levels(key, shape, cuts, -0.22, 0.18) * entries
    return jnp.clip(entries, min=-bound, max=bound).astype(kind)


def setup_inputs(seed: int = 0) -> dict:
    key_list = jax.random.split(jax.random.key(seed), 16)
    inputs = draw_inputs(jax.random.fold_in(key_list[15], 71), 0)
    cotangent = gaussian(key_list[1], (IMAGES, LEN, D), 1.0, 6.0, ((0, 8), (1, 4)))
    valid_len = draw_valid_len(jax.random.fold_in(key_list[15], 71), 0)
    ln1_gain = jnp.clip(1.0 + 0.18 * jax.random.normal(key_list[3], (D,), jnp.float32), 0.099609375, 1.8984375).astype(jnp.bfloat16)
    ln1_bias = gaussian(key_list[4], (D,), 0.5, 3.0, ((0, 8),))
    w_qkv = draw_w_qkv(jax.random.fold_in(key_list[15], 71), 0)
    b_qv = gaussian(key_list[6], (2 * D,), 0.5, 3.0, ((0, 8),))
    w_out = gaussian(key_list[7], (D, D), (HD // 8) ** -0.5, 2.0, ((0, 8),))
    b_out = gaussian(key_list[8], (D,), 0.5, 3.0, ((0, 8),))
    ln2_gain = jnp.clip(1.0 + 0.18 * jax.random.normal(key_list[9], (D,), jnp.float32), 0.099609375, 1.8984375).astype(jnp.bfloat16)
    ln2_bias = gaussian(key_list[10], (D,), 0.5, 3.0, ((0, 8),))
    w_up = gaussian(key_list[11], (D, FF), D ** -0.5, 0.1875, ((0, 8),))
    b_up = gaussian(key_list[12], (FF,), 0.5, 3.0, ((0, 8),))
    w_down = gaussian(key_list[13], (FF, D), FF ** -0.5, 0.09375, ((0, 8),))
    b_down = gaussian(key_list[14], (D,), 0.5, 3.0, ((0, 8),))
    return dict(inputs=inputs, cotangent=cotangent, valid_len=valid_len, ln1_gain=ln1_gain, ln1_bias=ln1_bias, w_qkv=w_qkv, b_qv=b_qv, w_out=w_out, b_out=b_out, ln2_gain=ln2_gain, ln2_bias=ln2_bias, w_up=w_up, b_up=b_up, w_down=w_down, b_down=b_down)


EPSILON = 1e-05
ROOT_HALF = 0.7071067811865476
GAUSS_DENSITY = 0.3989422804014327
NEG_LARGE = -1e+30

def norm_forward(values, gain_vec, shift_vec):
    mean_val = lax.optimization_barrier(jnp.mean(values, axis=-1, keepdims=True))
    centred = values - mean_val
    inv_std = lax.rsqrt(lax.optimization_barrier(jnp.mean(centred * centred, axis=-1, keepdims=True)) + EPSILON)
    normed = centred * inv_std
    return (normed, inv_std, normed * gain_vec.astype(jnp.float32) + shift_vec.astype(jnp.float32))

def norm_backward(upstream, normed, inv_std, gain_vec):
    scaled = upstream * gain_vec.astype(jnp.float32)
    first_mean = lax.optimization_barrier(jnp.mean(scaled, axis=-1, keepdims=True))
    second_mean = lax.optimization_barrier(jnp.mean(scaled * normed, axis=-1, keepdims=True))
    return inv_std * (scaled - first_mean - normed * second_mean)

def gelu_value(preact):
    return 0.5 * preact * (1.0 + lax.erf(preact * ROOT_HALF))

def gelu_slope(preact):
    return 0.5 * (1.0 + lax.erf(preact * ROOT_HALF)) + preact * jnp.exp(-0.5 * preact * preact) * GAUSS_DENSITY

def scores_of(queries, keys, valid_count, factor):
    logits = jnp.einsum('qhe,khe->hqk', queries.astype(jnp.float32), keys.astype(jnp.float32)) * factor
    key_live = lax.iota(jnp.int32, keys.shape[0]) < valid_count
    return jnp.where(key_live[None, None, :], logits, NEG_LARGE)

def attend_forward(queries, keys, values_in, valid_count, factor):
    logits = scores_of(queries, keys, valid_count, factor)
    row_max = lax.optimization_barrier(jnp.max(logits, axis=-1, keepdims=True))
    log_total = row_max + jnp.log(lax.optimization_barrier(jnp.sum(jnp.exp(logits - row_max), axis=-1, keepdims=True)))
    weights = jnp.exp(logits - log_total).astype(jnp.bfloat16)
    output = jnp.einsum('hqk,khe->qhe', weights.astype(jnp.float32), values_in.astype(jnp.float32))
    return (output.astype(jnp.bfloat16), log_total)

def attend_backward(queries, keys, values_in, output, log_total, d_output, valid_count, factor):
    logits = scores_of(queries, keys, valid_count, factor)
    attn_probs = jnp.exp(logits - log_total)
    probs_bf = attn_probs.astype(jnp.bfloat16)
    d_values = jnp.einsum('hqk,qhe->khe', probs_bf.astype(jnp.float32), d_output.astype(jnp.float32)).astype(jnp.bfloat16)
    d_probs = jnp.einsum('qhe,khe->hqk', d_output.astype(jnp.float32), values_in.astype(jnp.float32))
    row_dot = lax.optimization_barrier(jnp.sum(d_output.astype(jnp.float32) * output.astype(jnp.float32), axis=-1))
    d_logits = (factor * attn_probs * (d_probs - jnp.transpose(row_dot)[:, :, None])).astype(jnp.bfloat16)
    d_queries = jnp.einsum('hqk,khe->qhe', d_logits.astype(jnp.float32), keys.astype(jnp.float32)).astype(jnp.bfloat16)
    d_keys = jnp.einsum('hqk,qhe->khe', d_logits.astype(jnp.float32), queries.astype(jnp.float32)).astype(jnp.bfloat16)
    return (d_queries, d_keys, d_values)

def reference(inputs, cotangent, valid_len, ln1_gain, ln1_bias, w_qkv, b_qv, w_out, b_out, ln2_gain, ln2_bias, w_up, b_up, w_down, b_down):
    factor = 1.0 / math.sqrt(HD)
    qkv_bias = jnp.concatenate([b_qv[:D], jnp.zeros((D,), jnp.bfloat16), b_qv[D:]]).astype(jnp.float32)
    params = (ln1_gain, ln1_bias, w_qkv, b_qv, w_out, b_out, ln2_gain, ln2_bias, w_up, b_up, w_down, b_down)

    def one_image(totals, element):
        image_in, image_cot, live_count = element
        token_rows = image_in.astype(jnp.float32)
        normed_one, inv_one, pre_one = norm_forward(token_rows, ln1_gain, ln1_bias)
        hidden_one = pre_one.astype(jnp.bfloat16)
        projected = (jnp.dot(hidden_one, w_qkv, preferred_element_type=jnp.float32) + qkv_bias).astype(jnp.bfloat16)
        split_heads = projected.reshape(LEN, 3, H, HD)
        attended, log_total = attend_forward(split_heads[:, 0], split_heads[:, 1], split_heads[:, 2], live_count, factor)
        merged = attended.reshape(LEN, D)
        residual = token_rows + jnp.dot(merged, w_out, preferred_element_type=jnp.float32) + b_out.astype(jnp.float32)
        normed_two, inv_two, pre_two = norm_forward(residual, ln2_gain, ln2_bias)
        hidden_two = pre_two.astype(jnp.bfloat16)
        preact = jnp.dot(hidden_two, w_up, preferred_element_type=jnp.float32) + b_up.astype(jnp.float32)
        activated = gelu_value(preact).astype(jnp.bfloat16)
        result = residual + jnp.dot(activated, w_down, preferred_element_type=jnp.float32) + b_down.astype(jnp.float32)
        cot_rows = image_cot.astype(jnp.float32)
        grad_down = jnp.dot(activated.T, image_cot, preferred_element_type=jnp.float32)
        bias_down = lax.optimization_barrier(jnp.sum(cot_rows, axis=0))
        d_preact = jnp.dot(image_cot, w_down.T, preferred_element_type=jnp.float32) * gelu_slope(preact)
        grad_hidden = d_preact.astype(jnp.bfloat16)
        grad_up = jnp.dot(hidden_two.T, grad_hidden, preferred_element_type=jnp.float32)
        bias_up = lax.optimization_barrier(jnp.sum(d_preact, axis=0))
        d_second = jnp.dot(grad_hidden, w_up.T, preferred_element_type=jnp.float32)
        second_gain = lax.optimization_barrier(jnp.sum(d_second * normed_two, axis=0))
        second_shift = lax.optimization_barrier(jnp.sum(d_second, axis=0))
        d_residual = cot_rows + norm_backward(d_second, normed_two, inv_two, ln2_gain)
        res_bf = d_residual.astype(jnp.bfloat16)
        grad_out = jnp.dot(merged.T, res_bf, preferred_element_type=jnp.float32)
        bias_out = lax.optimization_barrier(jnp.sum(d_residual, axis=0))
        d_merged = jnp.dot(res_bf, w_out.T, preferred_element_type=jnp.float32).astype(jnp.bfloat16)
        d_queries, d_keys, d_values = attend_backward(split_heads[:, 0], split_heads[:, 1], split_heads[:, 2], attended, log_total, d_merged.reshape(LEN, H, HD), live_count, factor)
        d_proj = jnp.stack([d_queries, d_keys, d_values], axis=1).reshape(LEN, 3 * D)
        grad_qkv = jnp.dot(hidden_one.T, d_proj, preferred_element_type=jnp.float32)
        summed = lax.optimization_barrier(jnp.sum(d_proj.astype(jnp.float32), axis=0))
        bias_qv = jnp.concatenate([summed[:D], summed[2 * D:]])
        d_first = jnp.dot(d_proj, w_qkv.T, preferred_element_type=jnp.float32)
        first_gain = lax.optimization_barrier(jnp.sum(d_first * normed_one, axis=0))
        first_shift = lax.optimization_barrier(jnp.sum(d_first, axis=0))
        d_image = (d_residual + norm_backward(d_first, normed_one, inv_one, ln1_gain)).astype(jnp.bfloat16)
        image_grads = (first_gain, first_shift, grad_qkv, bias_qv, grad_out, bias_out, second_gain, second_shift, grad_up, bias_up, grad_down, bias_down)
        return (jax.tree.map(jnp.add, totals, image_grads), (result.astype(jnp.bfloat16), d_image))
    zeros = tuple((jnp.zeros(param_arr.shape, jnp.float32) for param_arr in params))
    totals, stacked = lax.scan(one_image, zeros, (inputs, cotangent, valid_len.astype(jnp.int32)))
    outputs, d_inputs = stacked
    return (outputs, d_inputs, totals[0], totals[1], totals[2], totals[3], totals[4], totals[5], totals[6], totals[7], totals[8], totals[9], totals[10], totals[11])
```

```python
import math

import jax
import jax.numpy as jnp
from jax import lax
from jax.sharding import PartitionSpec as P

HD = 64


EPSILON = 1e-05
ROOT_HALF = 0.7071067811865476
GAUSS_DENSITY = 0.3989422804014327
NEG_LARGE = -1e30


def norm_forward(values, gain_vec, shift_vec):
    mean_val = jnp.mean(values, axis=-1, keepdims=True)
    centred = values - mean_val
    inv_std = lax.rsqrt(jnp.mean(centred * centred, axis=-1, keepdims=True) + EPSILON)
    normed = centred * inv_std
    return (normed, inv_std, normed * gain_vec.astype(jnp.float32) + shift_vec.astype(jnp.float32))


def norm_backward(upstream, normed, inv_std, gain_vec):
    scaled = upstream * gain_vec.astype(jnp.float32)
    first_mean = jnp.mean(scaled, axis=-1, keepdims=True)
    second_mean = jnp.mean(scaled * normed, axis=-1, keepdims=True)
    return inv_std * (scaled - first_mean - normed * second_mean)


def gelu_value(preact):
    return 0.5 * preact * (1.0 + lax.erf(preact * ROOT_HALF))


def gelu_slope(preact):
    return (
        0.5 * (1.0 + lax.erf(preact * ROOT_HALF))
        + preact * jnp.exp(-0.5 * preact * preact) * GAUSS_DENSITY
    )


def against(left_mat, right_mat):
    return lax.dot_general(
        left_mat, right_mat, (((1,), (1,)), ((), ())), preferred_element_type=jnp.float32
    )


def outer_sum(left_mat, right_mat):
    return lax.dot_general(
        left_mat, right_mat, (((0,), (0,)), ((), ())), preferred_element_type=jnp.float32
    )


def scores_of(queries, keys, valid_count, factor):
    logits = jnp.einsum("qhe,khe->hqk", queries, keys, preferred_element_type=jnp.float32) * factor
    key_live = lax.iota(jnp.int32, keys.shape[0]) < valid_count
    return jnp.where(key_live[None, None, :], logits, NEG_LARGE)


def attend_forward(queries, keys, values_in, valid_count, factor):
    logits = scores_of(queries, keys, valid_count, factor)
    row_max = jnp.max(logits, axis=-1, keepdims=True)
    log_total = row_max + jnp.log(jnp.sum(jnp.exp(logits - row_max), axis=-1, keepdims=True))
    weights = jnp.exp(logits - log_total).astype(jnp.bfloat16)
    output = jnp.einsum("hqk,khe->qhe", weights, values_in, preferred_element_type=jnp.float32)
    return (output.astype(jnp.bfloat16), log_total)


def attend_backward(queries, keys, values_in, output, log_total, d_output, valid_count, factor):
    logits = scores_of(queries, keys, valid_count, factor)
    attn_probs = jnp.exp(logits - log_total)
    probs_bf = attn_probs.astype(jnp.bfloat16)
    d_values = jnp.einsum(
        "hqk,qhe->khe", probs_bf, d_output, preferred_element_type=jnp.float32
    ).astype(jnp.bfloat16)
    d_probs = jnp.einsum("qhe,khe->hqk", d_output, values_in, preferred_element_type=jnp.float32)
    row_dot = jnp.sum(d_output.astype(jnp.float32) * output.astype(jnp.float32), axis=-1)
    d_logits = (factor * attn_probs * (d_probs - jnp.transpose(row_dot)[:, :, None])).astype(
        jnp.bfloat16
    )
    d_queries = jnp.einsum(
        "hqk,khe->qhe", d_logits, keys, preferred_element_type=jnp.float32
    ).astype(jnp.bfloat16)
    d_keys = jnp.einsum(
        "hqk,qhe->khe", d_logits, queries, preferred_element_type=jnp.float32
    ).astype(jnp.bfloat16)
    return (d_queries, d_keys, d_values)


def seq_total(part):
    share = lax.psum_scatter(part, "seq", scatter_dimension=0, tiled=True)
    return lax.all_gather(share, "seq", axis=0, tiled=True).astype(jnp.float32)


def attention_forward(projected, valid_len, images, factor):
    local_width = projected.shape[1] // 3
    heads = local_width // HD
    packed = projected.reshape(images, -1, 3, heads, HD)

    def one(element):
        rows, live = element
        return attend_forward(rows[:, 0], rows[:, 1], rows[:, 2], live, factor)

    attended, totals = lax.map(one, (packed, valid_len))
    return attended.reshape(-1, local_width), totals


def attention_backward(projected, valid_len, attended, saved, d_heads, images, factor):
    local_width = projected.shape[1] // 3
    heads = local_width // HD
    packed = projected.reshape(images, -1, 3, heads, HD)

    def one(element):
        rows, live, out, total, grad = element
        return jnp.stack(
            attend_backward(
                rows[:, 0], rows[:, 1], rows[:, 2], out, total, grad, live, factor
            ),
            axis=1,
        )

    shape = (images, packed.shape[1], heads, HD)
    grads = lax.map(
        one, (packed, valid_len, attended.reshape(shape), saved, d_heads.reshape(shape))
    )
    return grads.reshape(-1, 3 * local_width)


def shards(
    inputs,
    cotangent,
    valid_len,
    ln1_gain,
    ln1_bias,
    w_qkv,
    b_qv,
    w_out,
    b_out,
    ln2_gain,
    ln2_bias,
    w_up,
    b_up,
    w_down,
    b_down,
):
    images, shard_len, width = inputs.shape
    groups = lax.axis_size("seq")
    owners = lax.axis_size("dp")
    my_seq = lax.axis_index("seq")
    my_dp = lax.axis_index("dp")
    local_width = width // groups
    heads_local = local_width // HD
    rows_owned = w_qkv.shape[0]
    hidden_local = w_down.shape[0]
    hidden_all = hidden_local * owners
    tokens = images * shard_len
    factor = 1.0 / math.sqrt(HD)
    bf16, f32 = jnp.bfloat16, jnp.float32

    tokens_all = lax.all_gather(inputs, "seq", axis=1, tiled=True)
    qkv_slice = lax.dynamic_slice_in_dim(
        w_qkv.reshape(rows_owned, 3, groups, local_width), my_seq, 1, axis=2
    ).reshape(rows_owned, 3 * local_width)
    qkv_cols = lax.all_gather(qkv_slice, "dp", axis=0, tiled=True)
    vectors = (ln1_gain, ln1_bias, b_out, ln2_gain, ln2_bias, b_down, b_qv)
    packed = lax.all_gather(jnp.concatenate(vectors), "dp", axis=0, tiled=False)
    pieces = []
    offset = 0
    for vec in vectors:
        pieces.append(packed[:, offset : offset + vec.shape[0]].reshape(-1))
        offset += vec.shape[0]
    gain_one, bias_one, out_bias, gain_two, bias_two, down_bias, qv_bias = pieces
    out_full = lax.all_gather(w_out, "dp", axis=0, tiled=True)
    up_cols = lax.all_to_all(w_up, "dp", split_axis=1, concat_axis=0, tiled=True)
    cot_all = lax.all_gather(
        cotangent.reshape(tokens, width), "dp", axis=0, tiled=True
    )

    seq_len = tokens_all.shape[1]
    rows_all = tokens_all.reshape(images * seq_len, width)
    hidden_one = norm_forward(rows_all.astype(f32), gain_one, bias_one)[2].astype(bf16)
    qkv_bias = jnp.concatenate(
        [qv_bias[:width], jnp.zeros((width,), bf16), qv_bias[width:]]
    ).reshape(3, groups, local_width)
    qkv_bias = lax.dynamic_slice_in_dim(qkv_bias, my_seq, 1, axis=1).reshape(-1).astype(f32)
    projected = (
        jnp.dot(hidden_one, qkv_cols, preferred_element_type=f32) + qkv_bias
    ).astype(bf16)
    attended, saved = attention_forward(projected, valid_len, images, factor)
    merged = lax.all_to_all(
        attended.reshape(images, seq_len, local_width),
        "seq",
        split_axis=1,
        concat_axis=2,
        tiled=True,
    )
    merged_rows = merged.reshape(tokens, width)
    token_rows = inputs.reshape(tokens, width).astype(f32)
    residual = (
        token_rows
        + jnp.dot(merged_rows, out_full, preferred_element_type=f32)
        + out_bias.astype(f32)
    )
    normed_two, inv_two, pre_two = norm_forward(residual, gain_two, bias_two)

    hidden_two = lax.all_gather(pre_two.astype(bf16), "dp", axis=0, tiled=True)
    d_act = against(cot_all, w_down)
    preact = jnp.dot(hidden_two, up_cols, preferred_element_type=f32) + b_up.astype(f32)
    activated = gelu_value(preact).astype(bf16)
    d_preact = d_act * gelu_slope(preact)
    grad_hidden = d_preact.astype(bf16)
    d_second = lax.psum_scatter(
        against(grad_hidden, up_cols).astype(bf16), "dp", scatter_dimension=0, tiled=True
    ).astype(f32)
    mlp_part = jnp.dot(activated, w_down, preferred_element_type=f32).astype(bf16)
    mlp_sum = lax.psum_scatter(mlp_part, "dp", scatter_dimension=0, tiled=True).astype(f32)
    outputs = (residual + mlp_sum + down_bias.astype(f32)).astype(bf16)
    outputs = outputs.reshape(images, shard_len, width)
    grad_down = seq_total(outer_sum(activated, cot_all).astype(bf16))
    grad_up = lax.all_to_all(
        outer_sum(hidden_two, grad_hidden).astype(bf16),
        "dp",
        split_axis=0,
        concat_axis=1,
        tiled=True,
    )
    grad_up = seq_total(grad_up)
    bias_up = jnp.sum(d_preact, axis=0)

    cot_rows = cotangent.reshape(tokens, width).astype(f32)
    bias_down = jnp.sum(cot_rows, axis=0)
    second_gain = jnp.sum(d_second * normed_two, axis=0)
    second_shift = jnp.sum(d_second, axis=0)
    d_residual = cot_rows + norm_backward(d_second, normed_two, inv_two, gain_two)
    res_bf = d_residual.astype(bf16)
    d_merged = against(res_bf, out_full).astype(bf16).reshape(images, shard_len, width)
    d_heads = lax.all_to_all(d_merged, "seq", split_axis=2, concat_axis=1, tiled=True)
    bias_out = jnp.sum(d_residual, axis=0)
    grad_out = lax.psum_scatter(
        outer_sum(merged_rows, res_bf).astype(bf16), "dp", scatter_dimension=0, tiled=True
    )
    grad_out = seq_total(grad_out)

    d_proj = attention_backward(
        projected,
        valid_len,
        attended,
        saved,
        d_heads.reshape(images * seq_len, local_width),
        images,
        factor,
    )
    d_first = lax.psum_scatter(
        against(d_proj, qkv_cols).astype(bf16).reshape(images, seq_len, width),
        "seq",
        scatter_dimension=1,
        tiled=True,
    )
    d_first = d_first.reshape(tokens, width).astype(f32)
    grad_qkv = lax.psum_scatter(
        outer_sum(hidden_one, d_proj).astype(bf16), "dp", scatter_dimension=0, tiled=True
    )
    grad_qkv = lax.all_gather(grad_qkv, "seq", axis=0, tiled=False)
    grad_qkv = (
        grad_qkv.reshape(groups, rows_owned, 3, local_width)
        .transpose(1, 2, 0, 3)
        .reshape(rows_owned, 3 * width)
        .astype(f32)
    )
    summed = jnp.sum(d_proj.astype(f32), axis=0).reshape(3, 1, local_width)
    bias_qv = lax.dynamic_update_slice(
        jnp.zeros((2, groups, local_width), f32),
        jnp.concatenate([summed[:1], summed[2:]], axis=0),
        (0, my_seq, 0),
    ).reshape(-1)
    normed_one, inv_one, _ = norm_forward(token_rows, gain_one, bias_one)
    first_gain = jnp.sum(d_first * normed_one, axis=0)
    first_shift = jnp.sum(d_first, axis=0)
    d_inputs = (
        (d_residual + norm_backward(d_first, normed_one, inv_one, gain_one))
        .astype(bf16)
        .reshape(images, shard_len, width)
    )

    def owned(*parts):
        sums = lax.psum(jnp.concatenate(parts), ("dp", "seq"))
        result = []
        start = 0
        for part in parts:
            share = part.shape[0] // owners
            result.append(lax.dynamic_slice_in_dim(sums, start + my_dp * share, share))
            start += part.shape[0]
        return result

    own_second_gain, own_second_shift, own_out, own_down = owned(
        second_gain, second_shift, bias_out, bias_down
    )
    own_up = lax.psum(bias_up, "seq")
    own_gain, own_shift, own_qv = owned(first_gain, first_shift, bias_qv)
    return (
        outputs,
        d_inputs,
        own_gain,
        own_shift,
        grad_qkv,
        own_qv,
        grad_out,
        own_out,
        own_second_gain,
        own_second_shift,
        grad_up,
        own_up,
        grad_down,
        own_down,
    )


def solution(mesh):
    placed = (
        P("dp", "seq", None),
        P("dp", "seq", None),
        P("dp"),
        P("dp"),
        P("dp"),
        P("dp", None),
        P("dp"),
        P("dp", None),
        P("dp"),
        P("dp"),
        P("dp"),
        P("dp", None),
        P("dp"),
        P("dp", None),
        P("dp"),
    )
    return jax.shard_map(
        shards,
        mesh=mesh,
        in_specs=placed,
        out_specs=(
            P("dp", "seq", None),
            P("dp", "seq", None),
            P("dp"),
            P("dp"),
            P("dp", None),
            P("dp"),
            P("dp", None),
            P("dp"),
            P("dp"),
            P("dp"),
            P("dp", None),
            P("dp"),
            P("dp", None),
            P("dp"),
        ),
        check_vma=False,
    )
```

```python
import functools
import math

import jax
import jax.numpy as jnp
from jax import lax
from jax.experimental import pallas as pl
from jax.experimental.pallas import tpu as pltpu
from jax.sharding import PartitionSpec as P

HD = 64


EPSILON = 1e-05
ROOT_HALF = 0.7071067811865476
GAUSS_DENSITY = 0.3989422804014327
NEG_LARGE = -1e30


def norm_forward(values, gain_vec, shift_vec):
    mean_val = jnp.mean(values, axis=-1, keepdims=True)
    centred = values - mean_val
    inv_std = lax.rsqrt(jnp.mean(centred * centred, axis=-1, keepdims=True) + EPSILON)
    normed = centred * inv_std
    return (normed, inv_std, normed * gain_vec.astype(jnp.float32) + shift_vec.astype(jnp.float32))


def norm_backward(upstream, normed, inv_std, gain_vec):
    scaled = upstream * gain_vec.astype(jnp.float32)
    first_mean = jnp.mean(scaled, axis=-1, keepdims=True)
    second_mean = jnp.mean(scaled * normed, axis=-1, keepdims=True)
    return inv_std * (scaled - first_mean - normed * second_mean)


def gelu_value(preact):
    return 0.5 * preact * (1.0 + lax.erf(preact * ROOT_HALF))


def gelu_slope(preact):
    return (
        0.5 * (1.0 + lax.erf(preact * ROOT_HALF))
        + preact * jnp.exp(-0.5 * preact * preact) * GAUSS_DENSITY
    )


def against(left_mat, right_mat):
    return lax.dot_general(
        left_mat, right_mat, (((1,), (1,)), ((), ())), preferred_element_type=jnp.float32
    )


def outer_sum(left_mat, right_mat):
    return lax.dot_general(
        left_mat, right_mat, (((0,), (0,)), ((), ())), preferred_element_type=jnp.float32
    )


def forward_kernel(factor, chunk, live_ref, q_ref, k_ref, v_ref, out_ref, lse_ref):
    rows = q_ref.shape[0]
    live = live_ref[...] > 0.0
    values = v_ref[...].astype(jnp.float32).T.astype(jnp.bfloat16)
    for start in range(0, rows, chunk):
        parts = []
        for head in range(q_ref.shape[1] // HD):
            lanes = slice(head * HD, (head + 1) * HD)
            queries = q_ref[start : start + chunk, lanes] * jnp.bfloat16(factor)
            logits = jnp.where(live, against(k_ref[:, lanes], queries), NEG_LARGE)
            top = jnp.max(logits, axis=0, keepdims=True)
            powers = jnp.exp(logits - top)
            total = jnp.sum(powers, axis=0, keepdims=True)
            lse_ref[head : head + 1, start : start + chunk] = top + jnp.log(total)
            probs = (powers * (1.0 / total)).astype(jnp.bfloat16)
            parts.append(jnp.dot(values[lanes], probs, preferred_element_type=jnp.float32))
        merged = jnp.concatenate(parts, axis=0).T
        out_ref[start : start + chunk, :] = merged.astype(jnp.bfloat16)


def backward_kernel(
    factor,
    chunk,
    live_ref,
    q_ref,
    k_ref,
    v_ref,
    out_ref,
    lse_ref,
    grad_ref,
    dq_ref,
    dk_ref,
    dv_ref,
    dk_sum,
    dv_sum,
):
    rows = q_ref.shape[0]
    live = live_ref[...] > 0.0
    keys_t = k_ref[...].astype(jnp.float32).T.astype(jnp.bfloat16)
    for start in range(0, rows, chunk):
        span = slice(start, start + chunk)
        grads = grad_ref[span, :]
        dots = (grads.astype(jnp.float32) * out_ref[span, :].astype(jnp.float32)).T
        parts = []
        for head in range(q_ref.shape[1] // HD):
            lanes = slice(head * HD, (head + 1) * HD)
            queries = q_ref[span, lanes]
            grad = grads[:, lanes]
            delta = jnp.sum(dots[lanes], axis=0, keepdims=True) * factor
            logits = jnp.where(
                live, against(k_ref[:, lanes], queries * jnp.bfloat16(factor)), NEG_LARGE
            )
            probs = jnp.exp(logits - lse_ref[head : head + 1, span])
            d_probs = against(v_ref[:, lanes], grad * jnp.bfloat16(factor))
            d_logits = (probs * (d_probs - delta)).astype(jnp.bfloat16)
            dv_new = jnp.dot(
                probs.astype(jnp.bfloat16), grad, preferred_element_type=jnp.float32
            )
            dk_new = jnp.dot(d_logits, queries, preferred_element_type=jnp.float32)
            if start == 0:
                dv_sum[:, lanes] = dv_new
                dk_sum[:, lanes] = dk_new
            else:
                dv_sum[:, lanes] += dv_new
                dk_sum[:, lanes] += dk_new
            parts.append(jnp.dot(keys_t[lanes], d_logits, preferred_element_type=jnp.float32))
        dq_ref[span, :] = jnp.concatenate(parts, axis=0).T.astype(jnp.bfloat16)
    dk_ref[...] = dk_sum[...].astype(jnp.bfloat16)
    dv_ref[...] = dv_sum[...].astype(jnp.bfloat16)


def attention_specs(rows, pairs):
    live = pl.BlockSpec((None, rows, 1), lambda i, j: (i, 0, 0))
    part = [
        pl.BlockSpec((rows, 2 * HD), functools.partial(lambda c, i, j: (i, c * pairs + j), c))
        for c in range(3)
    ]
    lse = pl.BlockSpec((None, None, 2, rows), lambda i, j: (i, j, 0, 0))
    return live, part, lse


def chunk_of(rows):
    return 384 if rows % 384 == 0 else 128


def attention_forward(projected, live, images, factor):
    rows = projected.shape[0] // images
    pairs = projected.shape[1] // (6 * HD)
    live_spec, part, lse_spec = attention_specs(rows, pairs)
    work = images * pairs * 2 * rows * rows
    return pl.pallas_call(
        functools.partial(forward_kernel, factor, chunk_of(rows)),
        grid=(images, pairs),
        in_specs=[live_spec, *part],
        out_specs=[part[0], lse_spec],
        out_shape=[
            jax.ShapeDtypeStruct((images * rows, pairs * 2 * HD), jnp.bfloat16),
            jax.ShapeDtypeStruct((images, pairs, 2, rows), jnp.float32),
        ],
        compiler_params=pltpu.CompilerParams(vmem_limit_bytes=48 * 2**20),
        cost_estimate=pl.CostEstimate(
            flops=4 * work * HD, bytes_accessed=8 * projected.size // 3, transcendentals=work
        ),
        name="attention_forward",
    )(live, projected, projected, projected)


def attention_backward(projected, live, attended, lse, d_heads, images, factor):
    rows = projected.shape[0] // images
    pairs = projected.shape[1] // (6 * HD)
    live_spec, part, lse_spec = attention_specs(rows, pairs)
    work = images * pairs * 2 * rows * rows
    shape = jax.ShapeDtypeStruct((images * rows, pairs * 2 * HD), jnp.bfloat16)
    return pl.pallas_call(
        functools.partial(backward_kernel, factor, chunk_of(rows)),
        grid=(images, pairs),
        in_specs=[live_spec, *part, part[0], lse_spec, part[0]],
        out_specs=[part[0]] * 3,
        out_shape=[shape] * 3,
        scratch_shapes=[pltpu.VMEM((rows, 2 * HD), jnp.float32)] * 2,
        compiler_params=pltpu.CompilerParams(vmem_limit_bytes=48 * 2**20),
        cost_estimate=pl.CostEstimate(
            flops=10 * work * HD, bytes_accessed=16 * projected.size // 3, transcendentals=work
        ),
        name="attention_backward",
    )(live, projected, projected, projected, attended, lse, d_heads)


def shift(block, step):
    groups = lax.axis_size("seq")
    pairs = [(place, (place + step) % groups) for place in range(groups)]
    return lax.ppermute(block, "seq", pairs)


def turned(array, by):
    return lax.dynamic_slice_in_dim(jnp.concatenate([array, array]), by, array.shape[0])


def pad_rows(array, rows, axis=0):
    widths = [(0, 0)] * array.ndim
    widths[axis] = (0, rows - array.shape[axis])
    return jnp.pad(array, widths)


def extra_rows(vectors, owners, width):
    row = jnp.concatenate([vec.reshape(owners, 1, -1) for vec in vectors], axis=2)
    row = jnp.pad(row, ((0, 0), (0, 15), (0, width - row.shape[2])))
    return row.astype(jnp.bfloat16)


def shards(
    inputs,
    cotangent,
    valid_len,
    ln1_gain,
    ln1_bias,
    w_qkv,
    b_qv,
    w_out,
    b_out,
    ln2_gain,
    ln2_bias,
    w_up,
    b_up,
    w_down,
    b_down,
):
    images, shard_len, width = inputs.shape
    groups = lax.axis_size("seq")
    owners = lax.axis_size("dp")
    my_seq = lax.axis_index("seq")
    local_width = width // groups
    rows_owned = w_qkv.shape[0]
    hidden_local = w_down.shape[0]
    factor = 1.0 / math.sqrt(HD)
    bf16, f32 = jnp.bfloat16, jnp.float32

    step = math.lcm(16, 128 // math.gcd(groups, 128))
    padded = -(-shard_len // step) * step
    mlp_len = -(-shard_len // 16) * 16
    rows = images * padded
    seq_len = groups * padded

    inputs_pad = pad_rows(inputs, padded, 1)
    slots = [inputs_pad] + [shift(inputs_pad, k) for k in range(1, groups)]
    vectors = (ln1_gain, ln1_bias, b_out, ln2_gain, ln2_bias, b_down, b_qv)
    packed = lax.all_gather(jnp.concatenate(vectors), "dp", axis=0, tiled=False)
    pieces = []
    offset = 0
    for vec in vectors:
        pieces.append(packed[:, offset : offset + vec.shape[0]].reshape(-1))
        offset += vec.shape[0]
    gain_one, bias_one, out_bias, gain_two, bias_two, down_bias, qv_bias = pieces
    qkv_slice = lax.dynamic_slice_in_dim(
        w_qkv.reshape(rows_owned, 3, groups, local_width), my_seq, 1, axis=2
    ).reshape(rows_owned, 3 * local_width)
    qkv_cols = lax.all_gather(qkv_slice, "dp", axis=0, tiled=True)
    out_full = turned(lax.all_gather(w_out, "dp", axis=0, tiled=True), my_seq * local_width)
    up_cols = lax.all_to_all(w_up, "dp", split_axis=1, concat_axis=0, tiled=True)
    cot_mine = pad_rows(cotangent, mlp_len, 1).reshape(images * mlp_len, width)
    cot_all = lax.all_gather(cot_mine, "dp", axis=0, tiled=True)

    place = jnp.arange(seq_len)
    source = lax.rem(my_seq - place // padded + groups, groups)
    within = place % padded
    token_id = jnp.where(within < shard_len, source * shard_len + within, groups * shard_len)
    live = (token_id[None, :] < valid_len[:, None]).astype(f32)[:, :, None]

    rows_all = jnp.concatenate(slots, axis=1).reshape(images * seq_len, width)
    normed_all, _, pre_all = norm_forward(rows_all.astype(f32), gain_one, bias_one)
    hidden_one = pre_all.astype(bf16)
    qkv_bias = jnp.concatenate(
        [qv_bias[:width], jnp.zeros((width,), bf16), qv_bias[width:]]
    ).reshape(3, groups, local_width)
    qkv_bias = lax.dynamic_slice_in_dim(qkv_bias, my_seq, 1, axis=1).reshape(-1).astype(f32)
    projected = (
        jnp.dot(hidden_one, qkv_cols, preferred_element_type=f32) + qkv_bias
    ).astype(bf16)
    attended, lse = attention_forward(projected, live, images, factor)
    by_slot = attended.reshape(images, groups, padded, local_width)
    heads = [by_slot[:, 0]] + [shift(by_slot[:, k], -k) for k in range(1, groups)]
    merged_rows = jnp.concatenate(heads, axis=2).reshape(rows, width)
    token_rows = inputs_pad.reshape(rows, width).astype(f32)
    residual = (
        token_rows
        + jnp.dot(merged_rows, out_full, preferred_element_type=f32)
        + out_bias.astype(f32)
    )
    normed_two, inv_two, pre_two = norm_forward(residual, gain_two, bias_two)

    def to_mlp(array):
        return array.reshape(images, padded, width)[:, :mlp_len].reshape(-1, width)

    def from_mlp(array):
        whole = array.astype(f32).reshape(images, mlp_len, width)
        return pad_rows(whole, padded, 1).reshape(rows, width)

    def scatter(array):
        blocks = array.reshape(owners, images * mlp_len, width)
        return lax.psum_scatter(blocks, "dp", scatter_dimension=0, tiled=False)

    hidden_two = lax.all_gather(to_mlp(pre_two.astype(bf16)), "dp", axis=0, tiled=True)
    d_act = against(cot_all, w_down)
    preact = jnp.dot(hidden_two, up_cols, preferred_element_type=f32) + b_up.astype(f32)
    activated = gelu_value(preact).astype(bf16)
    d_preact = d_act * gelu_slope(preact)
    grad_hidden = d_preact.astype(bf16)
    d_second = from_mlp(scatter(against(grad_hidden, up_cols).astype(bf16)))
    mlp_part = jnp.dot(activated, w_down, preferred_element_type=f32).astype(bf16)
    mlp_sum = from_mlp(scatter(mlp_part))
    outputs = (residual + mlp_sum + down_bias.astype(f32)).astype(bf16)
    outputs = outputs.reshape(images, padded, width)[:, :shard_len]
    bias_up = jnp.sum(d_preact, axis=0)
    bias_row = jnp.pad(bias_up[None, :], ((0, 15), (0, width - hidden_local)))
    grad_down = jnp.concatenate([outer_sum(activated, cot_all), bias_row]).astype(bf16)
    grad_up = lax.all_to_all(
        outer_sum(hidden_two, grad_hidden).astype(bf16),
        "dp",
        split_axis=0,
        concat_axis=1,
        tiled=True,
    )
    grad_down, grad_up = lax.psum((grad_down, grad_up), "seq")
    own_up = grad_down[hidden_local, :hidden_local].astype(f32)
    grad_down = grad_down[:hidden_local].astype(f32)
    grad_up = grad_up.astype(f32)

    cot_rows = from_mlp(cot_mine)
    bias_down = jnp.sum(cot_rows, axis=0)
    second_gain = jnp.sum(d_second * normed_two, axis=0)
    second_shift = jnp.sum(d_second, axis=0)
    d_residual = cot_rows + norm_backward(d_second, normed_two, inv_two, gain_two)
    res_bf = d_residual.astype(bf16)
    d_merged = against(res_bf, out_full).astype(bf16).reshape(images, padded, width)
    grads = [
        d_merged[:, :, k * local_width : (k + 1) * local_width] for k in range(groups)
    ]
    grads = [grads[0]] + [shift(grads[k], k) for k in range(1, groups)]
    d_heads = jnp.concatenate(grads, axis=1).reshape(images * seq_len, local_width)
    bias_out = jnp.sum(d_residual, axis=0)
    grad_out = turned(
        outer_sum(merged_rows, res_bf).astype(bf16), (groups - my_seq) * local_width
    ).reshape(owners, rows_owned, width)
    small = extra_rows((second_gain, second_shift, bias_out, bias_down), owners, width)
    grad_out = lax.psum_scatter(
        jnp.concatenate([grad_out, small], axis=1), "dp", scatter_dimension=0, tiled=False
    )
    grad_out = lax.psum(grad_out, "seq").astype(f32)
    small = grad_out[rows_owned, : 4 * rows_owned].reshape(4, rows_owned)
    own_second_gain, own_second_shift, own_out, own_down = small
    grad_out = grad_out[:rows_owned]

    d_proj = jnp.concatenate(
        attention_backward(projected, live, attended, lse, d_heads, images, factor), axis=1
    )
    d_part = against(d_proj, qkv_cols)
    first_gain = jnp.sum(d_part * normed_all, axis=0)
    first_shift = jnp.sum(d_part, axis=0)
    by_slot = d_part.astype(bf16).reshape(images, groups, padded, width)
    d_first = by_slot[:, 0].astype(f32)
    for k in range(1, groups):
        d_first += shift(by_slot[:, k], -k).astype(f32)
    d_first = d_first.reshape(rows, width)
    summed = jnp.sum(d_proj.astype(f32), axis=0).reshape(3, 1, local_width)
    bias_qv = lax.dynamic_update_slice(
        jnp.zeros((2, groups, local_width), f32),
        jnp.concatenate([summed[:1], summed[2:]], axis=0),
        (0, my_seq, 0),
    ).reshape(-1)
    small = extra_rows((first_gain, first_shift, bias_qv), owners, 3 * local_width)
    grad_qkv = outer_sum(hidden_one, d_proj).astype(bf16)
    grad_qkv = jnp.concatenate(
        [grad_qkv.reshape(owners, rows_owned, 3 * local_width), small], axis=1
    )
    grad_qkv = lax.psum_scatter(grad_qkv, "dp", scatter_dimension=0, tiled=False)
    grad_qkv = lax.all_gather(grad_qkv, "seq", axis=0, tiled=False).astype(f32)
    small = jnp.sum(grad_qkv[:, rows_owned], axis=0)
    own_gain = small[:rows_owned]
    own_shift = small[rows_owned : 2 * rows_owned]
    own_qv = small[2 * rows_owned : 4 * rows_owned]
    grad_qkv = (
        grad_qkv[:, :rows_owned]
        .reshape(groups, rows_owned, 3, local_width)
        .transpose(1, 2, 0, 3)
        .reshape(rows_owned, 3 * width)
    )
    normed_one, inv_one, _ = norm_forward(token_rows, gain_one, bias_one)
    d_inputs = (d_residual + norm_backward(d_first, normed_one, inv_one, gain_one)).astype(bf16)
    d_inputs = d_inputs.reshape(images, padded, width)[:, :shard_len]
    return (
        outputs,
        d_inputs,
        own_gain,
        own_shift,
        grad_qkv,
        own_qv,
        grad_out,
        own_out,
        own_second_gain,
        own_second_shift,
        grad_up,
        own_up,
        grad_down,
        own_down,
    )


def solution(mesh):
    placed = (
        P("dp", "seq", None),
        P("dp", "seq", None),
        P("dp"),
        P("dp"),
        P("dp"),
        P("dp", None),
        P("dp"),
        P("dp", None),
        P("dp"),
        P("dp"),
        P("dp"),
        P("dp", None),
        P("dp"),
        P("dp", None),
        P("dp"),
    )
    return jax.shard_map(
        shards,
        mesh=mesh,
        in_specs=placed,
        out_specs=(
            P("dp", "seq", None),
            P("dp", "seq", None),
            P("dp"),
            P("dp"),
            P("dp", None),
            P("dp"),
            P("dp", None),
            P("dp"),
            P("dp"),
            P("dp"),
            P("dp", None),
            P("dp"),
            P("dp", None),
            P("dp"),
        ),
        check_vma=False,
    )
```

```python
import functools
import math

import jax
import jax.numpy as jnp
from jax import lax
from jax.experimental import pallas as pl
from jax.experimental.pallas import tpu as pltpu
from jax.sharding import PartitionSpec as P

HD = 64


EPSILON = 1e-05
ROOT_HALF = 0.7071067811865476
GAUSS_DENSITY = 0.3989422804014327
NEG_LARGE = -1e30


def norm_forward(values, gain_vec, shift_vec):
    mean_val = jnp.mean(values, axis=-1, keepdims=True)
    centred = values - mean_val
    inv_std = lax.rsqrt(jnp.mean(centred * centred, axis=-1, keepdims=True) + EPSILON)
    normed = centred * inv_std
    return (normed, inv_std, normed * gain_vec.astype(jnp.float32) + shift_vec.astype(jnp.float32))


def norm_backward(upstream, normed, inv_std, gain_vec):
    scaled = upstream * gain_vec.astype(jnp.float32)
    first_mean = jnp.mean(scaled, axis=-1, keepdims=True)
    second_mean = jnp.mean(scaled * normed, axis=-1, keepdims=True)
    return inv_std * (scaled - first_mean - normed * second_mean)


def gelu_value(preact):
    return 0.5 * preact * (1.0 + lax.erf(preact * ROOT_HALF))


def gelu_slope(preact):
    return (
        0.5 * (1.0 + lax.erf(preact * ROOT_HALF))
        + preact * jnp.exp(-0.5 * preact * preact) * GAUSS_DENSITY
    )


def against(left_mat, right_mat):
    return lax.dot_general(
        left_mat, right_mat, (((1,), (1,)), ((), ())), preferred_element_type=jnp.float32
    )


def outer_sum(left_mat, right_mat):
    return lax.dot_general(
        left_mat, right_mat, (((0,), (0,)), ((), ())), preferred_element_type=jnp.float32
    )


def forward_kernel(factor, chunk, live_ref, q_ref, k_ref, v_ref, out_ref, lse_ref):
    rows = q_ref.shape[0]
    live = live_ref[...] > 0.0
    values = v_ref[...].astype(jnp.float32).T.astype(jnp.bfloat16)
    for start in range(0, rows, chunk):
        parts = []
        for head in range(q_ref.shape[1] // HD):
            lanes = slice(head * HD, (head + 1) * HD)
            queries = q_ref[start : start + chunk, lanes] * jnp.bfloat16(factor)
            logits = jnp.where(live, against(k_ref[:, lanes], queries), NEG_LARGE)
            top = jnp.max(logits, axis=0, keepdims=True)
            powers = jnp.exp(logits - top)
            total = jnp.sum(powers, axis=0, keepdims=True)
            lse_ref[head : head + 1, start : start + chunk] = top + jnp.log(total)
            probs = (powers * (1.0 / total)).astype(jnp.bfloat16)
            parts.append(jnp.dot(values[lanes], probs, preferred_element_type=jnp.float32))
        merged = jnp.concatenate(parts, axis=0).T
        out_ref[start : start + chunk, :] = merged.astype(jnp.bfloat16)


def backward_kernel(
    factor,
    chunk,
    live_ref,
    q_ref,
    k_ref,
    v_ref,
    out_ref,
    lse_ref,
    grad_ref,
    dq_ref,
    dk_ref,
    dv_ref,
    dk_sum,
    dv_sum,
):
    rows = q_ref.shape[0]
    live = live_ref[...] > 0.0
    keys_t = k_ref[...].astype(jnp.float32).T.astype(jnp.bfloat16)
    for start in range(0, rows, chunk):
        span = slice(start, start + chunk)
        grads = grad_ref[span, :]
        dots = (grads.astype(jnp.float32) * out_ref[span, :].astype(jnp.float32)).T
        parts = []
        for head in range(q_ref.shape[1] // HD):
            lanes = slice(head * HD, (head + 1) * HD)
            queries = q_ref[span, lanes]
            grad = grads[:, lanes]
            delta = jnp.sum(dots[lanes], axis=0, keepdims=True) * factor
            logits = jnp.where(
                live, against(k_ref[:, lanes], queries * jnp.bfloat16(factor)), NEG_LARGE
            )
            probs = jnp.exp(logits - lse_ref[head : head + 1, span])
            d_probs = against(v_ref[:, lanes], grad * jnp.bfloat16(factor))
            d_logits = (probs * (d_probs - delta)).astype(jnp.bfloat16)
            dv_new = jnp.dot(
                probs.astype(jnp.bfloat16), grad, preferred_element_type=jnp.float32
            )
            dk_new = jnp.dot(d_logits, queries, preferred_element_type=jnp.float32)
            if start == 0:
                dv_sum[:, lanes] = dv_new
                dk_sum[:, lanes] = dk_new
            else:
                dv_sum[:, lanes] += dv_new
                dk_sum[:, lanes] += dk_new
            parts.append(jnp.dot(keys_t[lanes], d_logits, preferred_element_type=jnp.float32))
        dq_ref[span, :] = jnp.concatenate(parts, axis=0).T.astype(jnp.bfloat16)
    dk_ref[...] = dk_sum[...].astype(jnp.bfloat16)
    dv_ref[...] = dv_sum[...].astype(jnp.bfloat16)


def attention_specs(rows, pairs):
    live = pl.BlockSpec((None, rows, 1), lambda i, j: (i, 0, 0))
    part = [
        pl.BlockSpec((rows, 2 * HD), functools.partial(lambda c, i, j: (i, c * pairs + j), c))
        for c in range(3)
    ]
    lse = pl.BlockSpec((None, None, 2, rows), lambda i, j: (i, j, 0, 0))
    return live, part, lse


def chunk_of(rows):
    return 384 if rows % 384 == 0 else 128


def attention_forward(projected, live, images, factor):
    rows = projected.shape[0] // images
    pairs = projected.shape[1] // (6 * HD)
    live_spec, part, lse_spec = attention_specs(rows, pairs)
    work = images * pairs * 2 * rows * rows
    return pl.pallas_call(
        functools.partial(forward_kernel, factor, chunk_of(rows)),
        grid=(images, pairs),
        in_specs=[live_spec, *part],
        out_specs=[part[0], lse_spec],
        out_shape=[
            jax.ShapeDtypeStruct((images * rows, pairs * 2 * HD), jnp.bfloat16),
            jax.ShapeDtypeStruct((images, pairs, 2, rows), jnp.float32),
        ],
        compiler_params=pltpu.CompilerParams(vmem_limit_bytes=48 * 2**20),
        cost_estimate=pl.CostEstimate(
            flops=4 * work * HD, bytes_accessed=8 * projected.size // 3, transcendentals=work
        ),
        name="attention_forward",
    )(live, projected, projected, projected)


def attention_backward(projected, live, attended, lse, d_heads, images, factor):
    rows = projected.shape[0] // images
    pairs = projected.shape[1] // (6 * HD)
    live_spec, part, lse_spec = attention_specs(rows, pairs)
    work = images * pairs * 2 * rows * rows
    shape = jax.ShapeDtypeStruct((images * rows, pairs * 2 * HD), jnp.bfloat16)
    return pl.pallas_call(
        functools.partial(backward_kernel, factor, chunk_of(rows)),
        grid=(images, pairs),
        in_specs=[live_spec, *part, part[0], lse_spec, part[0]],
        out_specs=[part[0]] * 3,
        out_shape=[shape] * 3,
        scratch_shapes=[pltpu.VMEM((rows, 2 * HD), jnp.float32)] * 2,
        compiler_params=pltpu.CompilerParams(vmem_limit_bytes=48 * 2**20),
        cost_estimate=pl.CostEstimate(
            flops=10 * work * HD, bytes_accessed=16 * projected.size // 3, transcendentals=work
        ),
        name="attention_backward",
    )(live, projected, projected, projected, attended, lse, d_heads)


def shift(block, step):
    groups = lax.axis_size("seq")
    pairs = [(place, (place + step) % groups) for place in range(groups)]
    return lax.ppermute(block, "seq", pairs)


def exchange_sum(blocks):
    owners = blocks.shape[0]
    mine = lax.axis_index("dp")
    total = lax.dynamic_index_in_dim(blocks, mine, 0, keepdims=False).astype(jnp.float32)
    for step in range(1, owners):
        target = lax.rem(mine + step, owners)
        block = lax.dynamic_index_in_dim(blocks, target, 0, keepdims=False)
        pairs = [(place, (place + step) % owners) for place in range(owners)]
        total += lax.ppermute(block, "dp", pairs).astype(jnp.float32)
    return total


def turned(array, by):
    return lax.dynamic_slice_in_dim(jnp.concatenate([array, array]), by, array.shape[0])


def pad_rows(array, rows, axis=0):
    widths = [(0, 0)] * array.ndim
    widths[axis] = (0, rows - array.shape[axis])
    return jnp.pad(array, widths)


def extra_rows(vectors, owners, width):
    row = jnp.concatenate([vec.reshape(owners, 1, -1) for vec in vectors], axis=2)
    row = jnp.pad(row, ((0, 0), (0, 15), (0, width - row.shape[2])))
    return row.astype(jnp.bfloat16)


def shards(
    inputs,
    cotangent,
    valid_len,
    ln1_gain,
    ln1_bias,
    w_qkv,
    b_qv,
    w_out,
    b_out,
    ln2_gain,
    ln2_bias,
    w_up,
    b_up,
    w_down,
    b_down,
):
    images, shard_len, width = inputs.shape
    groups = lax.axis_size("seq")
    owners = lax.axis_size("dp")
    my_seq = lax.axis_index("seq")
    local_width = width // groups
    rows_owned = w_qkv.shape[0]
    hidden_local = w_down.shape[0]
    factor = 1.0 / math.sqrt(HD)
    bf16, f32 = jnp.bfloat16, jnp.float32

    step = math.lcm(16, 128 // math.gcd(groups, 128))
    padded = -(-shard_len // step) * step
    mlp_len = -(-shard_len // 16) * 16
    rows = images * padded
    seq_len = groups * padded

    inputs_pad = pad_rows(inputs, padded, 1)
    slots = [inputs_pad] + [shift(inputs_pad, k) for k in range(1, groups)]
    vectors = (ln1_gain, ln1_bias, b_out, ln2_gain, ln2_bias, b_down, b_qv)
    packed = lax.all_gather(jnp.concatenate(vectors), "dp", axis=0, tiled=False)
    pieces = []
    offset = 0
    for vec in vectors:
        pieces.append(packed[:, offset : offset + vec.shape[0]].reshape(-1))
        offset += vec.shape[0]
    gain_one, bias_one, out_bias, gain_two, bias_two, down_bias, qv_bias = pieces
    qkv_slice = lax.dynamic_slice_in_dim(
        w_qkv.reshape(rows_owned, 3, groups, local_width), my_seq, 1, axis=2
    ).reshape(rows_owned, 3 * local_width)
    qkv_cols = lax.all_gather(qkv_slice, "dp", axis=0, tiled=True)
    out_full = turned(lax.all_gather(w_out, "dp", axis=0, tiled=True), my_seq * local_width)
    up_cols = lax.all_to_all(w_up, "dp", split_axis=1, concat_axis=0, tiled=True)
    cot_mine = pad_rows(cotangent, mlp_len, 1).reshape(images * mlp_len, width)
    slots, cot_mine, up_cols = lax.optimization_barrier((slots, cot_mine, up_cols))
    cot_all = lax.all_gather(cot_mine, "dp", axis=0, tiled=True)

    place = jnp.arange(seq_len)
    source = lax.rem(my_seq - place // padded + groups, groups)
    within = place % padded
    token_id = jnp.where(within < shard_len, source * shard_len + within, groups * shard_len)
    live = (token_id[None, :] < valid_len[:, None]).astype(f32)[:, :, None]

    rows_all = jnp.concatenate(slots, axis=1).reshape(images * seq_len, width)
    normed_all, _, pre_all = norm_forward(rows_all.astype(f32), gain_one, bias_one)
    hidden_one = pre_all.astype(bf16)
    qkv_bias = jnp.concatenate(
        [qv_bias[:width], jnp.zeros((width,), bf16), qv_bias[width:]]
    ).reshape(3, groups, local_width)
    qkv_bias = lax.dynamic_slice_in_dim(qkv_bias, my_seq, 1, axis=1).reshape(-1).astype(f32)
    projected = (
        jnp.dot(hidden_one, qkv_cols, preferred_element_type=f32) + qkv_bias
    ).astype(bf16)
    attended, lse = attention_forward(projected, live, images, factor)
    by_slot = attended.reshape(images, groups, padded, local_width)
    heads = [by_slot[:, 0]] + [shift(by_slot[:, k], -k) for k in range(1, groups)]
    merged_rows = jnp.concatenate(heads, axis=2).reshape(rows, width)
    token_rows = inputs_pad.reshape(rows, width).astype(f32)
    residual = (
        token_rows
        + jnp.dot(merged_rows, out_full, preferred_element_type=f32)
        + out_bias.astype(f32)
    )
    normed_two, inv_two, pre_two = norm_forward(residual, gain_two, bias_two)

    def to_mlp(array):
        return array.reshape(images, padded, width)[:, :mlp_len].reshape(-1, width)

    def from_mlp(array):
        whole = array.astype(f32).reshape(images, mlp_len, width)
        return pad_rows(whole, padded, 1).reshape(rows, width)

    def scatter(array):
        blocks = array.reshape(owners, images * mlp_len, width)
        return lax.psum_scatter(blocks, "dp", scatter_dimension=0, tiled=False)

    hidden_two = lax.all_gather(to_mlp(pre_two.astype(bf16)), "dp", axis=0, tiled=True)
    d_act = against(cot_all, w_down)
    preact = jnp.dot(hidden_two, up_cols, preferred_element_type=f32) + b_up.astype(f32)
    activated = gelu_value(preact).astype(bf16)
    d_preact = d_act * gelu_slope(preact)
    grad_hidden = d_preact.astype(bf16)
    d_second = scatter(against(grad_hidden, up_cols).astype(bf16))
    mlp_part = jnp.dot(activated, w_down, preferred_element_type=f32).astype(bf16)
    bias_up = jnp.sum(d_preact, axis=0)
    bias_row = jnp.pad(bias_up[None, :], ((0, 15), (0, width - hidden_local)))
    grad_down = jnp.concatenate([outer_sum(activated, cot_all), bias_row]).astype(bf16)
    grad_up = lax.all_to_all(
        outer_sum(hidden_two, grad_hidden).astype(bf16),
        "dp",
        split_axis=0,
        concat_axis=1,
        tiled=True,
    )
    d_second, mlp_part, grad_down, grad_up = lax.optimization_barrier(
        (d_second, mlp_part, grad_down, grad_up)
    )
    d_second = from_mlp(d_second)
    grad_down, grad_up = lax.psum((grad_down, grad_up), "seq")

    cot_rows = from_mlp(cot_mine)
    bias_down = jnp.sum(cot_rows, axis=0)
    second_gain = jnp.sum(d_second * normed_two, axis=0)
    second_shift = jnp.sum(d_second, axis=0)
    d_residual = cot_rows + norm_backward(d_second, normed_two, inv_two, gain_two)
    res_bf = d_residual.astype(bf16)
    d_merged = against(res_bf, out_full).astype(bf16).reshape(images, padded, width)
    grads = [
        d_merged[:, :, k * local_width : (k + 1) * local_width] for k in range(groups)
    ]
    grads = [grads[0]] + [shift(grads[k], k) for k in range(1, groups)]
    d_heads = jnp.concatenate(grads, axis=1).reshape(images * seq_len, local_width)
    d_heads, mlp_part = lax.optimization_barrier((d_heads, mlp_part))
    mlp_sum = from_mlp(exchange_sum(mlp_part.reshape(owners, images * mlp_len, width)))
    outputs = (residual + mlp_sum + down_bias.astype(f32)).astype(bf16)
    outputs = outputs.reshape(images, padded, width)[:, :shard_len]
    bias_out = jnp.sum(d_residual, axis=0)
    grad_out = turned(
        outer_sum(merged_rows, res_bf).astype(bf16), (groups - my_seq) * local_width
    ).reshape(owners, rows_owned, width)
    small = extra_rows((second_gain, second_shift, bias_out, bias_down), owners, width)
    grad_out = jnp.concatenate([grad_out, small], axis=1)

    d_proj = jnp.concatenate(
        attention_backward(projected, live, attended, lse, d_heads, images, factor), axis=1
    )
    d_proj, grad_down, grad_up, grad_out = lax.optimization_barrier(
        (d_proj, grad_down, grad_up, grad_out)
    )
    grad_out = lax.psum_scatter(grad_out, "dp", scatter_dimension=0, tiled=False)
    d_part = against(d_proj, qkv_cols)
    first_gain = jnp.sum(d_part * normed_all, axis=0)
    first_shift = jnp.sum(d_part, axis=0)
    own_up = grad_down[hidden_local, :hidden_local].astype(f32)
    grad_down = grad_down[:hidden_local].astype(f32)
    grad_up = grad_up.astype(f32)
    by_slot = d_part.astype(bf16).reshape(images, groups, padded, width)
    d_first = by_slot[:, 0].astype(f32)
    for k in range(1, groups):
        d_first += shift(by_slot[:, k], -k).astype(f32)
    d_first = d_first.reshape(rows, width)
    summed = jnp.sum(d_proj.astype(f32), axis=0).reshape(3, 1, local_width)
    bias_qv = lax.dynamic_update_slice(
        jnp.zeros((2, groups, local_width), f32),
        jnp.concatenate([summed[:1], summed[2:]], axis=0),
        (0, my_seq, 0),
    ).reshape(-1)
    small = extra_rows((first_gain, first_shift, bias_qv), owners, 3 * local_width)
    grad_qkv = outer_sum(hidden_one, d_proj).astype(bf16)
    grad_qkv = jnp.concatenate(
        [grad_qkv.reshape(owners, rows_owned, 3 * local_width), small], axis=1
    )
    grad_qkv = lax.psum_scatter(grad_qkv, "dp", scatter_dimension=0, tiled=False)
    last = jnp.concatenate([grad_out, grad_qkv], axis=1)
    lasts = jnp.stack([last] + [shift(last, -k) for k in range(1, groups)]).astype(f32)
    grad_out = jnp.sum(lasts[:, :, :width], axis=0)
    small = grad_out[rows_owned, : 4 * rows_owned].reshape(4, rows_owned)
    own_second_gain, own_second_shift, own_out, own_down = small
    grad_out = grad_out[:rows_owned]
    grad_qkv = turned(lasts[:, :, width:], groups - my_seq)
    small = jnp.sum(grad_qkv[:, rows_owned], axis=0)
    own_gain = small[:rows_owned]
    own_shift = small[rows_owned : 2 * rows_owned]
    own_qv = small[2 * rows_owned : 4 * rows_owned]
    grad_qkv = (
        grad_qkv[:, :rows_owned]
        .reshape(groups, rows_owned, 3, local_width)
        .transpose(1, 2, 0, 3)
        .reshape(rows_owned, 3 * width)
    )
    normed_one, inv_one, _ = norm_forward(token_rows, gain_one, bias_one)
    d_inputs = (d_residual + norm_backward(d_first, normed_one, inv_one, gain_one)).astype(bf16)
    d_inputs = d_inputs.reshape(images, padded, width)[:, :shard_len]
    return (
        outputs,
        d_inputs,
        own_gain,
        own_shift,
        grad_qkv,
        own_qv,
        grad_out,
        own_out,
        own_second_gain,
        own_second_shift,
        grad_up,
        own_up,
        grad_down,
        own_down,
    )


def solution(mesh):
    placed = (
        P("dp", "seq", None),
        P("dp", "seq", None),
        P("dp"),
        P("dp"),
        P("dp"),
        P("dp", None),
        P("dp"),
        P("dp", None),
        P("dp"),
        P("dp"),
        P("dp"),
        P("dp", None),
        P("dp"),
        P("dp", None),
        P("dp"),
    )
    return jax.shard_map(
        shards,
        mesh=mesh,
        in_specs=placed,
        out_specs=(
            P("dp", "seq", None),
            P("dp", "seq", None),
            P("dp"),
            P("dp"),
            P("dp", None),
            P("dp"),
            P("dp", None),
            P("dp"),
            P("dp"),
            P("dp"),
            P("dp", None),
            P("dp"),
            P("dp", None),
            P("dp"),
        ),
        check_vma=False,
    )
```
